128 devices in a mesh: row: 8 (over y, x_lo), col: 16 (over z, x_hi, core).
Axes of the slice: x: 4 (x_hi: 2, x_lo: 2; x = x_hi * 2 + x_lo), y: 4, z: 4, core: 2. Of those that a mesh axis runs over, the one named last changes fastest.
Arguments:
- spectra: bfloat16 [16384, 1024], P(('row', 'col')), may hold values from -6 to 6
Outputs:
- coherence: float32 [2, 16384, 16384], P(None, 'row', 'col')
The draws below stay inside these ranges and needn't reach their ends.
All inputs are finite; a program needn't handle non-finite values.
Results may differ from the reference program's by a relative error of at most 0.0003.
Values may be sent and summed in bfloat16 or wider, within the bound.
No kernel may reach another device: no remote copies, remote signals or barrier semaphores. Data moves between devices by JAX's collectives and lax.ppermute only.
A program may use at most 128 MiB of HBM per device.

```python
import jax
import jax.numpy as jnp
from jax import lax

CHANNELS = 16384
TAPERS = 8
BINS = 64
SPEC = 1024


def block_scale(stream_key, dims, pieces, least, high):
    def one(axis_at, parts):
        heights = jax.random.uniform(jax.random.fold_in(jax.random.fold_in(stream_key, 6), axis_at), (parts,), jnp.float32, least / len(pieces), high / len(pieces))
        return jnp.repeat(jnp.exp(heights), dims[axis_at] // parts).reshape((-1,) + (1,) * (len(dims) - axis_at - 1))

    factor_of = one(*pieces[0])
    for cut in pieces[1:]:
        factor_of = factor_of * one(*cut)
    return factor_of


def gaussian(key, dims, scale, limit, pieces=(), kind=jnp.bfloat16):
    values = jax.random.normal(key, dims, jnp.float32) * scale
    if len(pieces) > 0:
        values = block_scale(key, dims, pieces, -0.22, 0.18) * values
    return jnp.clip(values, min=-limit, max=limit).astype(kind)


def setup_inputs(seed: int = 0) -> dict:
    key_of = jax.random.split(jax.random.key(seed), 2)
    return {
        "spectra": gaussian(key_of[0], (CHANNELS, SPEC), 1.0, 6.0, ((0, 128),)),
    }


def reference(spectra):
    half = TAPERS * BINS
    turned = jnp.concatenate([-spectra[:, half:], spectra[:, :half]], axis=1)
    stacked = jnp.concatenate([spectra, turned], axis=0)
    squares = spectra.astype(jnp.float32)
    power = lax.optimization_barrier(jnp.sum(squares * squares, axis=1))
    root = jnp.sqrt(power)
    block = 1024
    count = CHANNELS // block

    def one_block(index):
        rows = lax.dynamic_slice_in_dim(spectra, index * block, block, 0)
        row_root = lax.dynamic_slice_in_dim(root, index * block, block, 0)
        cross = lax.dot_general(rows, stacked, (((1,), (1,)), ((), ())), preferred_element_type=jnp.float32)
        scale = row_root[:, None] * root[None, :]
        real_part = cross[:, :CHANNELS] / scale
        imag_part = cross[:, CHANNELS:] / scale
        return jnp.stack([real_part, imag_part], axis=0)
    blocks = lax.map(one_block, jnp.arange(count, dtype=jnp.int32))
    return jnp.transpose(blocks, (1, 0, 2, 3)).reshape(2, CHANNELS, CHANNELS)
```

```python
import functools

import jax
import jax.numpy as jnp
from jax import lax
from jax.experimental import pallas as pl
from jax.experimental.pallas import tpu as pltpu
from jax.sharding import PartitionSpec as P

TAPERS = 8
BINS = 64
HALF = TAPERS * BINS
SPEC = 2 * HALF
AXES = ("row", "col")
NT = (((1,), (1,)), ((), ()))
F32, BF16 = jnp.float32, jnp.bfloat16
SHARD = 128
TILE = 256


def place(i):
    row, col = divmod(i, 16)
    return (col // 2 % 2) * 2 + row % 2, row // 2, col // 4, col % 2


def number(x, y, z, core):
    return (y * 2 + x % 2) * 16 + z * 4 + (x // 2) * 2 + core


def moves(rule):
    return [(i, number(*rule(*place(i)))) for i in range(128)]


SWAP_CORE = moves(lambda x, y, z, c: (x, y, z, 1 - c))
ACROSS_X = moves(lambda x, y, z, c: ((x + 2) % 4, y, z, c))
Y_UP = moves(lambda x, y, z, c: (x, (y + 1) % 4, z, c))
Y_DOWN = moves(lambda x, y, z, c: (x, (y + 3) % 4, z, c))
Z_RINGS = [[z * 4 + r for z in range(4)] for r in range(4)]


def to_columns(flip):
    def rule(x, y, z, c):
        low = c ^ flip
        return 2 * (x % 2) + low, (y + 2 * (z % 2) + x // 2) % 4, y, z // 2

    return moves(rule)


COLS_A, COLS_B = to_columns(0), to_columns(1)


def send(value, pairs):
    return lax.ppermute(value, AXES, pairs)


def together(*values):
    return lax.optimization_barrier(values)


def pair(a, b):
    return jnp.concatenate([a, b], axis=0)


def spots():
    row, col = lax.axis_index("row"), lax.axis_index("col")
    return row % 2, col // 2 % 2, row // 2, col // 4, col % 2


def kernel(pos, a0, a1, a2, a3, c_own, c_up, c_down, c_far0, c_far1, out, a_all, b, turned, col_inv, sems):
    step = pl.program_id(0)
    low, q = pos[1], pos[2]

    def a_copy(j):
        src = (a0, a1, a2, a3)[j]
        return pltpu.make_async_copy(src, a_all.at[pl.ds(j * 512, 512)], sems.at[j])

    def b_copies():
        copies = []
        for n, (src, turn) in enumerate(((c_own, 0), (c_up, 3), (c_down, 1), (c_far0, 2), (c_far1, 2))):
            base = lax.rem(q + turn, 4) * (2 * SHARD)
            if n < 3:
                for m in range(2):
                    at = pl.multiple_of(base + (low if m == 0 else 1 - low) * SHARD, SHARD)
                    copies.append((src.at[pl.ds(m * SHARD, SHARD)], at))
            else:
                at = pl.multiple_of(base + (low if n == 3 else 1 - low) * SHARD, SHARD)
                copies.append((src, at))
        return [
            pltpu.make_async_copy(s, b.at[pl.ds(at, SHARD)], sems.at[4 + m])
            for m, (s, at) in enumerate(copies)
        ]

    @pl.when(step == 0)
    def _():
        for copy in b_copies():
            copy.start()
        for j in range(4):
            a_copy(j).start()
        for copy in b_copies():
            copy.wait()
        values = b[...]
        turned[:, :HALF] = -values[:, HALF:]
        turned[:, HALF:] = values[:, :HALF]
        squares = values.astype(F32)
        squares = squares * squares
        high = squares.astype(BF16)
        rest = (squares - high.astype(F32)).astype(BF16)
        ones = jnp.ones((8, SPEC), BF16)
        power = lax.dot_general(ones, high, NT, preferred_element_type=F32)
        power += lax.dot_general(ones, rest, NT, preferred_element_type=F32)
        col_inv[...] = 1.0 / jnp.sqrt(power)

    for j in range(4):
        @pl.when(step == 2 * j)
        def _():
            a_copy(j).wait()

    a = a_all[pl.ds(pl.multiple_of(step * TILE, TILE), TILE), :]
    values = a.astype(F32)
    row_inv = 1.0 / jnp.sqrt(jnp.sum(values * values, axis=1, keepdims=True))
    scale = col_inv[0:1, :]
    real = lax.dot_general(a, b[...], NT, preferred_element_type=F32)
    out[0, :, 0] = (real * row_inv * scale).reshape(2, SHARD, 1024)
    imag = lax.dot_general(a, turned[...], NT, preferred_element_type=F32)
    out[1, :, 0] = (imag * row_inv * scale).reshape(2, SHARD, 1024)


def coherence(pos, rows, cols):
    def place_out(step, pos):
        j = step // 2
        spot = pos[0] ^ jnp.where(j % 2 == 1, 1, 0) ^ jnp.where(j // 2 == 1, 2, 0)
        return 0, step % 2, spot, 0, 0

    anywhere = pl.BlockSpec(memory_space=pl.ANY)
    out = pl.pallas_call(
        kernel,
        grid_spec=pltpu.PrefetchScalarGridSpec(
            num_scalar_prefetch=1,
            grid=(8,),
            in_specs=[anywhere] * 9,
            out_specs=pl.BlockSpec((2, 2, 1, SHARD, 1024), place_out),
            scratch_shapes=[
                pltpu.VMEM((2048, SPEC), BF16),
                pltpu.VMEM((1024, SPEC), BF16),
                pltpu.VMEM((1024, SPEC), BF16),
                pltpu.VMEM((8, 1024), F32),
                pltpu.SemaphoreType.DMA((12,)),
            ],
        ),
        out_shape=jax.ShapeDtypeStruct((2, 4, 4, SHARD, 1024), F32),
        compiler_params=pltpu.CompilerParams(vmem_limit_bytes=40 * 2**20),
        cost_estimate=pl.CostEstimate(flops=8 * 2**30, bytes_accessed=22 * 2**20, transcendentals=4096),
        name="coherence",
    )(pos, *rows, *cols)
    return out.reshape(2, 2048, 1024)


def shards(x):
    low, high, y, z, core = spots()
    pos = jnp.stack([high * 2 + core, low, (y + 4 - z) % 4]).astype(jnp.int32)
    own = lax.all_gather(x, "col", axis=0, tiled=True, axis_index_groups=Z_RINGS)
    c0, c1, across = send(x, COLS_A), send(x, COLS_B), send(x, ACROSS_X)
    other = lax.all_gather(across, "col", axis=0, tiled=True, axis_index_groups=Z_RINGS)
    c_own = pair(c0, c1)
    c_up, c_down = send(c_own, Y_UP), send(c_own, Y_DOWN)
    c_up, c_down, own = together(c_up, c_down, own)
    far0, far1 = send(c_up[:SHARD], Y_UP), send(c_down[SHARD:], Y_DOWN)
    own_swapped = send(own, SWAP_CORE)
    other_swapped = send(other, SWAP_CORE)
    rows = (own, own_swapped, other, other_swapped)
    return coherence(pos, rows, (c_own, c_up, c_down, far0, far1))


def solution(mesh):
    return jax.shard_map(
        shards, mesh=mesh, in_specs=(P(AXES, None),), out_specs=P(None, "row", "col"), check_vma=False
    )
```

```python
import jax
import jax.numpy as jnp
from jax import lax
from jax.experimental import pallas as pl
from jax.experimental.pallas import tpu as pltpu
from jax.sharding import PartitionSpec as P

TAPERS = 8
BINS = 64
HALF = TAPERS * BINS
SPEC = 2 * HALF
AXES = ("row", "col")
NT = (((1,), (1,)), ((), ()))
F32, BF16 = jnp.float32, jnp.bfloat16
SHARD = 128
COLS = 8 * SHARD
WIDE = COLS // 2
OUT = (2, 4, 2, 2, SHARD, COLS)
TILE = 2 * SHARD


def place(i):
    row, col = divmod(i, 16)
    return (col // 2 % 2) * 2 + row % 2, row // 2, col // 4, col % 2


def number(x, y, z, core):
    return (y * 2 + x % 2) * 16 + z * 4 + (x // 2) * 2 + core


def moves(rule):
    return [(i, number(*rule(*place(i)))) for i in range(128)]


SWAP_CORE = moves(lambda x, y, z, c: (x, y, z, 1 - c))
ACROSS_X = moves(lambda x, y, z, c: ((x + 2) % 4, y, z, c))
Y_UP = moves(lambda x, y, z, c: (x, (y + 1) % 4, z, c))
Y_DOWN = moves(lambda x, y, z, c: (x, (y + 3) % 4, z, c))
Z_UP = moves(lambda x, y, z, c: (x, y, (z + 1) % 4, c))
Z_DOWN = moves(lambda x, y, z, c: (x, y, (z + 3) % 4, c))
Z_SPLIT = moves(lambda x, y, z, c: (x, y, (z + 1 + 2 * c) % 4, c))


def to_columns(flip):
    def rule(x, y, z, c):
        return 2 * (x % 2) + (x // 2 ^ flip), (y + z + 2 * c) % 4, y, z // 2

    return moves(rule)


COLS_A, COLS_B = to_columns(0), to_columns(1)


def piece_spot(y, z, core, high):
    low_z = (y - z + 4) % 2
    from_core = ((y - z - low_z + 8) // 2 + core) % 2
    return low_z * 4 + high * 2 + from_core


def send(value, pairs):
    return lax.ppermute(value, AXES, pairs)


def column_scale(b):
    squares = jnp.zeros((WIDE, 128), F32)
    for n in range(0, SPEC, 128):
        values = b[:, n : n + 128].astype(F32)
        squares += values * values
    power = lax.dot_general(
        jnp.ones((8, 128), F32), squares, NT, precision=lax.Precision.HIGHEST, preferred_element_type=F32
    )
    return 1.0 / jnp.sqrt(power)


def products(a, b, col_inv, high, out):
    turned = jnp.concatenate([a[:, HALF:], -a[:, :HALF]], axis=1)
    values = a.astype(F32)
    row_inv = 1.0 / jnp.sqrt(jnp.sum(values * values, axis=1, keepdims=True))
    for part, lhs in enumerate((a, turned)):
        cross = lax.dot_general(lhs, b, NT, preferred_element_type=F32)
        scaled = cross * row_inv * col_inv
        out[part, 0, high, 0] = scaled[:SHARD]
        out[part, 0, 1 - high, 0] = scaled[SHARD:]


def half_kernel(where, rows, swapped, *refs):
    pieces, (out, b, col_inv, sems) = refs[:4], refs[-4:]
    step = pl.program_id(0)

    @pl.when(step == 0)
    def _():
        copies = []
        for n, piece in enumerate(pieces):
            at = pl.ds(pl.multiple_of(where[4 + n] * SHARD, SHARD), SHARD)
            copies.append(pltpu.make_async_copy(piece, b.at[at, :], sems.at[n]))
        for copy in copies:
            copy.start()
        for copy in copies:
            copy.wait()
        col_inv[...] = column_scale(b)

    a = jnp.where(step < 3, rows[...], swapped[...])
    products(a, b[...], col_inv[0:1, :], where[2], out)


def half_call(where, rows, swapped, pieces, before, name):
    def place_out(step, where):
        n = lax.rem(step, 3)
        z = lax.rem(where[0] + jnp.where(n == 1, 3, jnp.where(n == 2, 1, 0)), 4)
        return 0, z, 0, where[1] ^ (step // 3), 0, where[3]

    vmem, anywhere = pl.BlockSpec(memory_space=pltpu.VMEM), pl.BlockSpec(memory_space=pl.ANY)
    in_specs = [
        pl.BlockSpec((TILE, SPEC), lambda step, where: (jnp.minimum(step, 2), 0)),
        pl.BlockSpec((TILE, SPEC), lambda step, where: (jnp.maximum(step - 3, 0), 0)),
    ] + [anywhere] * 4
    operands, aliases = (rows, swapped, *[in_hbm(piece) for piece in pieces]), {}
    if before is not None:
        aliases = {1 + len(operands): 0}
        operands = (*operands, before)
        in_specs.append(anywhere)
    return pl.pallas_call(
        half_kernel,
        grid_spec=pltpu.PrefetchScalarGridSpec(
            num_scalar_prefetch=1,
            grid=(6,),
            in_specs=in_specs,
            out_specs=[pl.BlockSpec((2, 1, 2, 1, SHARD, WIDE), place_out), vmem, vmem],
            scratch_shapes=[pltpu.SemaphoreType.DMA((4,))],
        ),
        out_shape=[
            jax.ShapeDtypeStruct(OUT, F32),
            pltpu.VMEM((WIDE, SPEC), BF16),
            pltpu.VMEM((8, WIDE), F32),
        ],
        input_output_aliases=aliases,
        compiler_params=pltpu.CompilerParams(vmem_limit_bytes=16 * 2**20),
        cost_estimate=pl.CostEstimate(flops=3 * 2**30, bytes_accessed=11 * 2**20, transcendentals=2048),
        name=name,
    )(where, *operands)


def facing_kernel(where, rows, swapped, b0, scale0, b1, scale1, before, out):
    step = pl.program_id(0)
    a = jnp.where(step < 2, rows[...], swapped[...])
    even = lax.rem(step, 2) == 0
    b = jnp.where(even, b0[...], b1[...])
    scale = jnp.where(even, scale0[0:1, :], scale1[0:1, :])
    products(a, b, scale, where[2], out)


def facing_call(where, rows, swapped, first, second, before):
    def place_out(step, where):
        return 0, lax.rem(where[0] + 2, 4), 0, where[1] ^ (step // 2), 0, where[3] ^ lax.rem(step, 2)

    vmem, anywhere = pl.BlockSpec(memory_space=pltpu.VMEM), pl.BlockSpec(memory_space=pl.ANY)
    whole = pl.BlockSpec((TILE, SPEC), lambda step, where: (0, 0))
    return pl.pallas_call(
        facing_kernel,
        grid_spec=pltpu.PrefetchScalarGridSpec(
            num_scalar_prefetch=1,
            grid=(4,),
            in_specs=[whole, whole, vmem, vmem, vmem, vmem, anywhere],
            out_specs=pl.BlockSpec((2, 1, 2, 1, SHARD, WIDE), place_out),
        ),
        out_shape=jax.ShapeDtypeStruct(OUT, F32),
        input_output_aliases={7: 0},
        compiler_params=pltpu.CompilerParams(vmem_limit_bytes=16 * 2**20),
        cost_estimate=pl.CostEstimate(flops=2**31, bytes_accessed=8 * 2**20, transcendentals=2048),
        name="facing_rows",
    )(where, rows, swapped, *[in_vmem(v) for v in (*first, *second)], before)


def in_vmem(value):
    return pltpu.with_memory_space_constraint(value, pltpu.VMEM)


def in_hbm(value):
    return pltpu.with_memory_space_constraint(value, pltpu.HBM)


def stack(*values):
    return jnp.stack(values).astype(jnp.int32)


def shards(x):
    row, col = lax.axis_index("row"), lax.axis_index("col")
    low, y, z, high, core = row % 2, row // 2, col // 4, col // 2 % 2, col % 2
    c0, c1, across = send(x, COLS_A), send(x, COLS_B), send(x, ACROSS_X)
    below, above = send(x, Z_UP), send(x, Z_DOWN)
    up0, down0 = send(c0, Y_UP), send(c0, Y_DOWN)
    c1, up0, down0, across, below, above = lax.optimization_barrier((c1, up0, down0, across, below, above))
    down1, up1 = send(c1, Y_DOWN), send(c1, Y_UP)
    below_across, above_across = send(across, Z_UP), send(across, Z_DOWN)
    down1, up1, below_across, above_across = lax.optimization_barrier((down1, up1, below_across, above_across))
    far0, far1 = send(up0, Y_UP), send(down1, Y_DOWN)
    from_below = jnp.concatenate([below, below_across], axis=0)
    from_above = jnp.concatenate([above, above_across], axis=0)
    facing = send(jnp.where(core == 0, from_below, from_above), Z_SPLIT)
    rows = jnp.concatenate([x, across, from_below, from_above], axis=0)
    swapped = send(rows, SWAP_CORE)

    def spots(*steps):
        return [piece_spot((y + up) % 4, z, core, high_x) % 4 for up, high_x in steps]

    near_half = (y + 3 - z + 4) % 2
    where = stack(z, core, high, near_half, *spots((3, low), (3, 1 - low), (1, low), (1, 1 - low)))
    out, *first = half_call(where, rows, swapped, (up0, up1, down0, down1), None, "near_columns")
    out, far0, far1, facing = lax.optimization_barrier((out, far0, far1, facing))
    facing_swapped = send(facing, SWAP_CORE)
    far_where = stack(z, core, high, 1 - near_half, *spots((0, low), (0, 1 - low), (2, low), (2, 1 - low)))
    out, *second = half_call(far_where, rows, swapped, (c0, c1, far0, far1), out, "far_columns")
    out = facing_call(where, facing, facing_swapped, first, second, out)
    return out.reshape(2, 4 * 4 * SHARD, COLS)


def solution(mesh):
    return jax.shard_map(
        shards, mesh=mesh, in_specs=(P(AXES, None),), out_specs=P(None, "row", "col"), check_vma=False
    )
```

```python
import jax
import jax.numpy as jnp
from jax import lax
from jax.experimental import pallas as pl
from jax.experimental.pallas import tpu as pltpu
from jax.sharding import PartitionSpec as P

TAPERS = 8
BINS = 64
HALF = TAPERS * BINS
SPEC = 2 * HALF
AXES = ("row", "col")
NT = (((1,), (1,)), ((), ()))
F32, BF16 = jnp.float32, jnp.bfloat16
SHARD = 128
COLS = 8 * SHARD
WIDE = COLS // 2
OUT = (2, 4, 2, 2, SHARD, COLS)
TILE = 2 * SHARD


def place(i):
    row, col = divmod(i, 16)
    return (col // 2 % 2) * 2 + row % 2, row // 2, col // 4, col % 2


def number(x, y, z, core):
    return (y * 2 + x % 2) * 16 + z * 4 + (x // 2) * 2 + core


def moves(rule):
    return [(i, number(*rule(*place(i)))) for i in range(128)]


SWAP_CORE = moves(lambda x, y, z, c: (x, y, z, 1 - c))
ACROSS_X = moves(lambda x, y, z, c: ((x + 2) % 4, y, z, c))
Y_UP = moves(lambda x, y, z, c: (x, (y + 1) % 4, z, c))
Y_DOWN = moves(lambda x, y, z, c: (x, (y + 3) % 4, z, c))
Z_UP = moves(lambda x, y, z, c: (x, y, (z + 1) % 4, c))
Z_DOWN = moves(lambda x, y, z, c: (x, y, (z + 3) % 4, c))
Z_SPLIT_CROSS = moves(lambda x, y, z, c: (x, y, (z + 1 + 2 * c) % 4, 1 - c))
Z_SPLIT = moves(lambda x, y, z, c: (x, y, (z + 1 + 2 * c) % 4, c))


def to_columns(flip):
    def rule(x, y, z, c):
        return 2 * (x % 2) + (x // 2 ^ flip), (y + z + 2 * c) % 4, y, z // 2

    return moves(rule)


COLS_A, COLS_B = to_columns(0), to_columns(1)


def piece_spot(y, z, core, high):
    low_z = (y - z + 4) % 2
    from_core = ((y - z - low_z + 8) // 2 + core) % 2
    return low_z * 4 + high * 2 + from_core


def send(value, pairs):
    return lax.ppermute(value, AXES, pairs)


def column_scale(b):
    squares = jnp.zeros((WIDE, 128), F32)
    for n in range(0, SPEC, 128):
        values = b[:, n : n + 128].astype(F32)
        squares += values * values
    power = lax.dot_general(
        jnp.ones((8, 128), F32), squares, NT, precision=lax.Precision.HIGHEST, preferred_element_type=F32
    )
    return 1.0 / jnp.sqrt(power)


def products(rows, swapped, columns, core, out):
    a = jnp.concatenate([rows, swapped], axis=0)
    turned = jnp.concatenate([a[:, HALF:], -a[:, :HALF]], axis=1)
    values = a.astype(F32)
    row_inv = 1.0 / jnp.sqrt(jnp.sum(values * values, axis=1, keepdims=True))
    for b, col_inv, at in columns:
        for part, lhs in enumerate((a, turned)):
            cross = lax.dot_general(lhs, b[...], NT, preferred_element_type=F32)
            scaled = cross * row_inv * col_inv[0:1, :]
            out[part, 0, 0, core, :, at] = scaled[:SHARD]
            out[part, 0, 0, 1 - core, :, at] = scaled[SHARD:]


def half_kernel(where, rows, swapped, *refs):
    out, b, col_inv, sems = refs[-4:]
    pieces = [ref.at[pl.ds(n, SHARD)] for ref in refs[:-4] if len(ref.shape) == 2 for n in range(0, ref.shape[0], SHARD)]

    @pl.when(pl.program_id(0) == 0)
    def _():
        spots = [pl.ds(pl.multiple_of(where[4 + n] * SHARD, SHARD), SHARD) for n in range(4)]
        copies = [pltpu.make_async_copy(pieces[n], b.at[spots[n], :], sems.at[n]) for n in range(4)]
        for copy in copies:
            copy.start()
        for copy in copies:
            copy.wait()
        col_inv[...] = column_scale(b)

    products(rows[...], swapped[...], ((b, col_inv, slice(None)),), where[2], out)


def z_of(step, where):
    return lax.rem(where[0] + jnp.where(step == 1, 3, jnp.where(step == 2, 1, jnp.where(step == 3, 2, 0))), 4)


SHARD_SPEC = pl.BlockSpec((SHARD, SPEC), lambda step, where: (step, 0))


def half_call(where, rows, swapped, pieces, before, name):
    def place_out(step, where):
        return 0, z_of(step, where), where[1], 0, 0, where[3]

    vmem, anywhere = pl.BlockSpec(memory_space=pltpu.VMEM), pl.BlockSpec(memory_space=pl.ANY)
    in_specs = [SHARD_SPEC, SHARD_SPEC] + [anywhere] * len(pieces)
    operands, aliases = (rows, swapped, *[in_hbm(piece) for piece in pieces]), {}
    if before is not None:
        aliases = {1 + len(operands): 0}
        operands = (*operands, before)
        in_specs.append(anywhere)
    return pl.pallas_call(
        half_kernel,
        grid_spec=pltpu.PrefetchScalarGridSpec(
            num_scalar_prefetch=1,
            grid=(4,),
            in_specs=in_specs,
            out_specs=[pl.BlockSpec((2, 1, 1, 2, SHARD, WIDE), place_out), vmem, vmem],
            scratch_shapes=[pltpu.SemaphoreType.DMA((4,))],
        ),
        out_shape=[
            jax.ShapeDtypeStruct(OUT, F32),
            (pltpu.HBM if before is None else jax.ShapeDtypeStruct)((WIDE, SPEC), BF16),
            jax.ShapeDtypeStruct((8, WIDE), F32),
        ],
        input_output_aliases=aliases,
        compiler_params=pltpu.CompilerParams(vmem_limit_bytes=16 * 2**20),
        cost_estimate=pl.CostEstimate(flops=2**31, bytes_accessed=7 * 2**20, transcendentals=2048),
        name=name,
    )(where, *operands)


def last_kernel(where, rows3, facing, swapped3, swapped_facing, b0, scale0, b1, scale1, before, out):
    near = pl.program_id(0) < 3
    rows = jnp.where(near, rows3[...], facing[...])
    swapped = jnp.where(near, swapped3[...], swapped_facing[...])
    at0 = pl.ds(pl.multiple_of(where[3] * WIDE, WIDE), WIDE)
    at1 = pl.ds(pl.multiple_of((1 - where[3]) * WIDE, WIDE), WIDE)
    products(rows, swapped, ((b0, scale0, at0), (b1, scale1, at1)), where[2], out)


def last_call(where, rows, first, second, before):
    def place_out(step, where):
        return 0, z_of(step, where), 1 - where[1], 0, 0, 0

    vmem, anywhere = pl.BlockSpec(memory_space=pltpu.VMEM), pl.BlockSpec(memory_space=pl.ANY)
    first_spec = pl.BlockSpec((WIDE, SPEC), lambda step, where: (0, 0))
    of_three = pl.BlockSpec((SHARD, SPEC), lambda step, where: (jnp.minimum(step, 2), 0))
    whole = pl.BlockSpec((SHARD, SPEC), lambda step, where: (0, 0))
    return pl.pallas_call(
        last_kernel,
        grid_spec=pltpu.PrefetchScalarGridSpec(
            num_scalar_prefetch=1,
            grid=(4,),
            in_specs=[of_three, whole, of_three, whole, first_spec, vmem, vmem, vmem, anywhere],
            out_specs=pl.BlockSpec((2, 1, 1, 2, SHARD, COLS), place_out),
        ),
        out_shape=jax.ShapeDtypeStruct(OUT, F32),
        input_output_aliases={9: 0},
        compiler_params=pltpu.CompilerParams(vmem_limit_bytes=16 * 2**20),
        cost_estimate=pl.CostEstimate(flops=2**32, bytes_accessed=12 * 2**20, transcendentals=2048),
        name="across_rows",
    )(where, *rows, in_hbm(first[0]), first[1], *second, before)


def in_hbm(value):
    return pltpu.with_memory_space_constraint(value, pltpu.HBM)


def stack(*values):
    return jnp.stack(values).astype(jnp.int32)


def together(*values):
    return lax.optimization_barrier(values)


def family(*shards):
    return jnp.concatenate(shards, axis=0)


def shards(x):
    row, col = lax.axis_index("row"), lax.axis_index("col")
    low, y, z, high, core = row % 2, row // 2, col // 4, col // 2 % 2, col % 2

    def places(half, *steps):
        return stack(z, high, core, half, *[piece_spot((y + up) % 4, z, core, hx) % 4 for up, hx in steps])

    near_half = (y - z + 3) % 2
    where = places(near_half, (3, low), (3, 1 - low), (1, low), (1, 1 - low))
    where_far = places(1 - near_half, (0, low), (0, 1 - low), (2, low), (2, 1 - low))
    a0, across, below, above, b0 = send(x, COLS_A), send(x, ACROSS_X), send(x, Z_UP), send(x, Z_DOWN), send(x, COLS_B)
    a0, b0 = together(a0, b0)
    own = family(a0, b0)
    up, down = send(own, Y_UP), send(own, Y_DOWN)
    facing = send(jnp.where(core == 0, below, above), Z_SPLIT)
    below_across, above_across = send(across, Z_UP), send(across, Z_DOWN)
    onward = jnp.where(core == 0, below_across, above_across)
    rows_across = family(across, below_across, above_across)
    up, down, facing, rows_across, onward, up_a, down_b = together(up, down, facing, rows_across, onward, up[:SHARD], down[SHARD:])
    far0, far1 = send(up_a, Y_UP), send(down_b, Y_DOWN)
    rows = family(x, below, above, facing)
    swapped = send(rows, SWAP_CORE)
    facing_across = send(onward, Z_SPLIT)
    out, *first = half_call(where, rows, swapped, (up, down), None, "own_rows_near")
    out, facing_across, far0, far1 = together(out, facing_across, far0, far1)
    swapped_across = send(rows_across, SWAP_CORE)
    facing_swapped = send(facing_across, SWAP_CORE)
    out, *second = half_call(where_far, rows, swapped, (own, far0, far1), out, "own_rows_far")
    out = last_call(where, (rows_across, facing_across, swapped_across, facing_swapped), first, second, out)
    return out.reshape(2, 4 * 4 * SHARD, COLS)


def solution(mesh):
    return jax.shard_map(
        shards, mesh=mesh, in_specs=(P(AXES, None),), out_specs=P(None, "row", "col"), check_vma=False
    )
```

```python
import jax
import jax.numpy as jnp
from jax import lax
from jax.experimental import pallas as pl
from jax.experimental.pallas import tpu as pltpu
from jax.sharding import PartitionSpec as P

TAPERS = 8
BINS = 64
HALF = TAPERS * BINS
SPEC = 2 * HALF
AXES = ("row", "col")
NT = (((1,), (1,)), ((), ()))
F32, BF16 = jnp.float32, jnp.bfloat16
SHARD = 128
COLS = 8 * SHARD
WIDE = COLS // 2
OUT = (2, 4, 2, 2, SHARD, COLS)
TILE = 2 * SHARD


def place(i):
    row, col = divmod(i, 16)
    return (col // 2 % 2) * 2 + row % 2, row // 2, col // 4, col % 2


def number(x, y, z, core):
    return (y * 2 + x % 2) * 16 + z * 4 + (x // 2) * 2 + core


def moves(rule):
    return [(i, number(*rule(*place(i)))) for i in range(128)]


SWAP_CORE = moves(lambda x, y, z, c: (x, y, z, 1 - c))
ACROSS_X = moves(lambda x, y, z, c: ((x + 2) % 4, y, z, c))
Y_UP = moves(lambda x, y, z, c: (x, (y + 1) % 4, z, c))
Y_DOWN = moves(lambda x, y, z, c: (x, (y + 3) % 4, z, c))
Z_UP = moves(lambda x, y, z, c: (x, y, (z + 1) % 4, c))
Z_DOWN = moves(lambda x, y, z, c: (x, y, (z + 3) % 4, c))
Y_SPLIT = moves(lambda x, y, z, c: (x, (y + 1 + 2 * c) % 4, z, c))
Z_SPLIT = moves(lambda x, y, z, c: (x, y, (z + 1 + 2 * c) % 4, c))


def to_columns(flip):
    def rule(x, y, z, c):
        return 2 * (x % 2) + (x // 2 ^ flip), (y + z + 2 * c) % 4, y, z // 2

    return moves(rule)


COLS_A, COLS_B = to_columns(0), to_columns(1)


def piece_spot(y, z, core, high):
    low_z = (y - z + 4) % 2
    from_core = ((y - z - low_z + 8) // 2 + core) % 2
    return low_z * 4 + high * 2 + from_core


def send(value, pairs):
    return lax.ppermute(value, AXES, pairs)


def column_scale(b):
    squares = jnp.zeros((WIDE, 128), F32)
    for n in range(0, SPEC, 128):
        values = b[:, n : n + 128].astype(F32)
        squares += values * values
    power = lax.dot_general(
        jnp.ones((8, 128), F32), squares, NT, precision=lax.Precision.HIGHEST, preferred_element_type=F32
    )
    return 1.0 / jnp.sqrt(power)


def products(rows, swapped, columns, core, out):
    a = jnp.concatenate([rows, swapped], axis=0)
    turned = jnp.concatenate([a[:, HALF:], -a[:, :HALF]], axis=1)
    values = a.astype(F32)
    row_inv = 1.0 / jnp.sqrt(jnp.sum(values * values, axis=1, keepdims=True))
    for b, col_inv, at in columns:
        for part, lhs in enumerate((a, turned)):
            cross = lax.dot_general(lhs, b[...], NT, preferred_element_type=F32)
            scaled = cross * row_inv * col_inv[0:1, :]
            n = rows.shape[0] // SHARD
            out[part, :, 0, core, :, at] = scaled[: n * SHARD].reshape(n, SHARD, -1)
            out[part, :, 0, 1 - core, :, at] = scaled[n * SHARD :].reshape(n, SHARD, -1)


def half_kernel(where, rows, swapped, *refs):
    out, b, col_inv, sems = refs[-4:]
    pieces = [ref.at[pl.ds(n, SHARD)] for ref in refs[:-4] if len(ref.shape) == 2 for n in range(0, ref.shape[0], SHARD)]

    @pl.when(pl.program_id(0) == 0)
    def _():
        spots = [pl.ds(pl.multiple_of(where[4 + n] * SHARD, SHARD), SHARD) for n in range(4)]
        copies = [pltpu.make_async_copy(pieces[n], b.at[spots[n], :], sems.at[n]) for n in range(4)]
        for copy in copies:
            copy.start()
        for copy in copies:
            copy.wait()
        col_inv[...] = column_scale(b)

    products(rows[...], swapped[...], ((b, col_inv, slice(None)),), where[2], out)


def z_of(step, where):
    return lax.rem(where[0] + jnp.where(step == 1, 3, jnp.where(step == 2, 1, jnp.where(step == 3, 2, 0))), 4)


def half_call(where, rows, swapped, pieces, before, name):
    def place_out(step, where):
        return 0, step, where[1], 0, 0, where[3]

    pair = pl.BlockSpec((TILE, SPEC), lambda step, where: (step, 0))
    vmem, anywhere = pl.BlockSpec(memory_space=pltpu.VMEM), pl.BlockSpec(memory_space=pl.ANY)
    in_specs = [pair, pair] + [anywhere] * len(pieces)
    operands, aliases = (rows, swapped, *[in_hbm(piece) for piece in pieces]), {}
    if before is not None:
        aliases = {1 + len(operands): 0}
        operands = (*operands, before)
        in_specs.append(anywhere)
    return pl.pallas_call(
        half_kernel,
        grid_spec=pltpu.PrefetchScalarGridSpec(
            num_scalar_prefetch=1,
            grid=(2,),
            in_specs=in_specs,
            out_specs=[pl.BlockSpec((2, 2, 1, 2, SHARD, WIDE), place_out), vmem, vmem],
            scratch_shapes=[pltpu.SemaphoreType.DMA((4,))],
        ),
        out_shape=[
            jax.ShapeDtypeStruct(OUT, F32),
            (pltpu.HBM if before is None else jax.ShapeDtypeStruct)((WIDE, SPEC), BF16),
            jax.ShapeDtypeStruct((8, WIDE), F32),
        ],
        input_output_aliases=aliases,
        compiler_params=pltpu.CompilerParams(vmem_limit_bytes=16 * 2**20),
        cost_estimate=pl.CostEstimate(flops=2**31, bytes_accessed=7 * 2**20, transcendentals=2048),
        name=name,
    )(where, *operands)


def last_kernel(where, rows3, facing, swapped3, swapped_facing, b0, scale0, b1, scale1, before, out):
    near = pl.program_id(0) < 3
    rows = jnp.where(near, rows3[...], facing[...])
    swapped = jnp.where(near, swapped3[...], swapped_facing[...])
    at0 = pl.ds(pl.multiple_of(where[3] * WIDE, WIDE), WIDE)
    at1 = pl.ds(pl.multiple_of((1 - where[3]) * WIDE, WIDE), WIDE)
    products(rows, swapped, ((b0, scale0, at0), (b1, scale1, at1)), where[2], out)


def last_call(where, rows, first, second, before):
    def place_out(step, where):
        return 0, z_of(step, where), 1 - where[1], 0, 0, 0

    vmem, anywhere = pl.BlockSpec(memory_space=pltpu.VMEM), pl.BlockSpec(memory_space=pl.ANY)
    first_spec = pl.BlockSpec((WIDE, SPEC), lambda step, where: (0, 0))
    of_three = pl.BlockSpec((SHARD, SPEC), lambda step, where: (jnp.minimum(step, 2), 0))
    whole = pl.BlockSpec((SHARD, SPEC), lambda step, where: (0, 0))
    return pl.pallas_call(
        last_kernel,
        grid_spec=pltpu.PrefetchScalarGridSpec(
            num_scalar_prefetch=1,
            grid=(4,),
            in_specs=[of_three, whole, of_three, whole, first_spec, vmem, vmem, vmem, anywhere],
            out_specs=pl.BlockSpec((2, 1, 1, 2, SHARD, COLS), place_out),
        ),
        out_shape=jax.ShapeDtypeStruct(OUT, F32),
        input_output_aliases={9: 0},
        compiler_params=pltpu.CompilerParams(vmem_limit_bytes=16 * 2**20),
        cost_estimate=pl.CostEstimate(flops=2**32, bytes_accessed=12 * 2**20, transcendentals=2048),
        name="across_rows",
    )(where, *rows, in_hbm(first[0]), first[1], *second, before)


def in_hbm(value):
    return pltpu.with_memory_space_constraint(value, pltpu.HBM)


def stack(*values):
    return jnp.stack(values).astype(jnp.int32)


def together(*values):
    return lax.optimization_barrier(values)


def family(*shards):
    return jnp.concatenate(shards, axis=0)


def by_z(z, own, below, above, facing):
    rows = jnp.zeros((4 * SHARD, SPEC), BF16)
    for shard, up in ((own, 0), (below, 3), (above, 1), (facing, 2)):
        rows = lax.dynamic_update_slice(rows, shard, ((z + up) % 4 * SHARD, 0))
    return rows


def shards(x):
    row, col = lax.axis_index("row"), lax.axis_index("col")
    low, y, z, high, core = row % 2, row // 2, col // 4, col // 2 % 2, col % 2

    def places(half, *steps):
        return stack(z, high, core, half, *[piece_spot((y + up) % 4, z, core, hx) % 4 for up, hx in steps])

    near_half = (y - z + 3) % 2
    where = places(near_half, (3, low), (3, 1 - low), (1, low), (1, 1 - low))
    where_far = places(1 - near_half, (0, low), (0, 1 - low), (2, low), (2, 1 - low))
    a0, across, below, above, b0 = send(x, COLS_A), send(x, ACROSS_X), send(x, Z_UP), send(x, Z_DOWN), send(x, COLS_B)
    a0, b0 = together(a0, b0)
    own = family(a0, b0)
    up, down = send(own, Y_UP), send(own, Y_DOWN)
    facing = send(jnp.where(core == 0, below, above), Z_SPLIT)
    below_across, above_across = send(across, Z_UP), send(across, Z_DOWN)
    onward = jnp.where(core == 0, below_across, above_across)
    rows_across = family(across, below_across, above_across)
    up, down, facing, rows_across, onward, far = together(up, down, facing, rows_across, onward, jnp.where(core == 0, up, down))
    far = send(far, Y_SPLIT)
    rows = by_z(z, x, below, above, facing)
    swapped = send(rows, SWAP_CORE)
    facing_across = send(onward, Z_SPLIT)
    out, *first = half_call(where, rows, swapped, (up, down), None, "own_rows_near")
    out, facing_across, far = together(out, facing_across, far)
    swapped_across = send(rows_across, SWAP_CORE)
    facing_swapped = send(facing_across, SWAP_CORE)
    out, *second = half_call(where_far, rows, swapped, (own, far), out, "own_rows_far")
    out = last_call(where, (rows_across, facing_across, swapped_across, facing_swapped), first, second, out)
    return out.reshape(2, 4 * 4 * SHARD, COLS)


def solution(mesh):
    return jax.shard_map(
        shards, mesh=mesh, in_specs=(P(AXES, None),), out_specs=P(None, "row", "col"), check_vma=False
    )
```

```python
import jax
import jax.numpy as jnp
from jax import lax
from jax.experimental import pallas as pl
from jax.experimental.pallas import tpu as pltpu
from jax.sharding import PartitionSpec as P

TAPERS = 8
BINS = 64
HALF = TAPERS * BINS
SPEC = 2 * HALF
AXES = ("row", "col")
NT = (((1,), (1,)), ((), ()))
F32, BF16 = jnp.float32, jnp.bfloat16
SHARD = 128
COLS = 8 * SHARD
WIDE = COLS // 2
OUT = (2, 4, 2, 2, SHARD, COLS)
TILE = 2 * SHARD


def place(i):
    row, col = divmod(i, 16)
    return (col // 2 % 2) * 2 + row % 2, row // 2, col // 4, col % 2


def number(x, y, z, core):
    return (y * 2 + x % 2) * 16 + z * 4 + (x // 2) * 2 + core


def moves(rule):
    return [(i, number(*rule(*place(i)))) for i in range(128)]


SWAP_CORE = moves(lambda x, y, z, c: (x, y, z, 1 - c))
Y_FIRST = moves(lambda x, y, z, c: (x, (y + 1 + 2 * c) % 4, z, c))
Y_SECOND = moves(lambda x, y, z, c: (x, (y + 3 + 2 * c) % 4, z, c))
Z_FIRST = moves(lambda x, y, z, c: (x, y, (z + 1 + 2 * c) % 4, c))
Z_SECOND = moves(lambda x, y, z, c: (x, y, (z + 3 + 2 * c) % 4, c))
ACROSS_X = moves(lambda x, y, z, c: ((x + 2) % 4, y, z, c))


def to_columns(flip):
    def rule(x, y, z, c):
        return 2 * (x % 2) + (x // 2 ^ flip), (y + z + 2 * c) % 4, y, z // 2

    return moves(rule)


COLS_A, COLS_B = to_columns(0), to_columns(1)


def piece_spot(y, z, core, high):
    low_z = (y - z + 4) % 2
    from_core = ((y - z - low_z + 8) // 2 + core) % 2
    return low_z * 4 + high * 2 + from_core


def send(value, pairs):
    return lax.ppermute(value, AXES, pairs)


def column_scale(b):
    squares = jnp.zeros((WIDE, 128), F32)
    for n in range(0, SPEC, 128):
        values = b[:, n : n + 128].astype(F32)
        squares += values * values
    power = lax.dot_general(
        jnp.ones((8, 128), F32), squares, NT, precision=lax.Precision.HIGHEST, preferred_element_type=F32
    )
    return 1.0 / jnp.sqrt(power)


def products(rows, swapped, columns, core, out):
    a = jnp.concatenate([rows, swapped], axis=0)
    turned = jnp.concatenate([a[:, HALF:], -a[:, :HALF]], axis=1)
    values = a.astype(F32)
    row_inv = 1.0 / jnp.sqrt(jnp.sum(values * values, axis=1, keepdims=True))
    for b, col_inv, at in columns:
        for part, lhs in enumerate((a, turned)):
            cross = lax.dot_general(lhs, b[...], NT, preferred_element_type=F32)
            scaled = cross * row_inv * col_inv[0:1, :]
            n = rows.shape[0] // SHARD
            out[part, :, 0, core, :, at] = scaled[: n * SHARD].reshape(n, SHARD, -1)
            out[part, :, 0, 1 - core, :, at] = scaled[n * SHARD :].reshape(n, SHARD, -1)


def half_kernel(where, rows, swapped, *refs):
    out, b, col_inv, sems = refs[-4:]
    pieces = [ref.at[pl.ds(n, SHARD)] for ref in refs[:-4] if len(ref.shape) == 2 for n in range(0, ref.shape[0], SHARD)]

    @pl.when(pl.program_id(0) == 0)
    def _():
        spots = [pl.ds(pl.multiple_of(where[4 + n] * SHARD, SHARD), SHARD) for n in range(4)]
        copies = [pltpu.make_async_copy(pieces[n], b.at[spots[n], :], sems.at[n]) for n in range(4)]
        for copy in copies:
            copy.start()
        for copy in copies:
            copy.wait()
        col_inv[...] = column_scale(b)

    products(rows[...], swapped[...], ((b, col_inv, slice(None)),), where[2], out)


def z_of(step, where):
    first = 3 - 2 * where[2]
    return lax.rem(where[0] + jnp.where(step == 1, first, jnp.where(step == 2, 4 - first, 2 * (step // 3))), 4)


def half_call(where, rows, swapped, pieces, before, name):
    def place_out(step, where):
        return 0, step, where[1], 0, 0, where[3]

    pair = pl.BlockSpec((TILE, SPEC), lambda step, where: (step, 0))
    vmem, anywhere = pl.BlockSpec(memory_space=pltpu.VMEM), pl.BlockSpec(memory_space=pl.ANY)
    in_specs = [pair, pair] + [anywhere] * len(pieces)
    operands, aliases = (rows, swapped, *[in_hbm(piece) for piece in pieces]), {}
    if before is not None:
        aliases = {1 + len(operands): 0}
        operands = (*operands, before)
        in_specs.append(anywhere)
    return pl.pallas_call(
        half_kernel,
        grid_spec=pltpu.PrefetchScalarGridSpec(
            num_scalar_prefetch=1,
            grid=(2,),
            in_specs=in_specs,
            out_specs=[pl.BlockSpec((2, 2, 1, 2, SHARD, WIDE), place_out), vmem, vmem],
            scratch_shapes=[pltpu.SemaphoreType.DMA((4,))],
        ),
        out_shape=[
            jax.ShapeDtypeStruct(OUT, F32),
            (pltpu.HBM if before is None else jax.ShapeDtypeStruct)((WIDE, SPEC), BF16),
            jax.ShapeDtypeStruct((8, WIDE), F32),
        ],
        input_output_aliases=aliases,
        compiler_params=pltpu.CompilerParams(vmem_limit_bytes=16 * 2**20),
        cost_estimate=pl.CostEstimate(flops=2**31, bytes_accessed=7 * 2**20, transcendentals=2048),
        name=name,
    )(where, *operands)


def last_kernel(where, rows3, facing, swapped3, swapped_facing, b0, scale0, b1, scale1, before, out):
    near = pl.program_id(0) < 3
    rows = jnp.where(near, rows3[...], facing[...])
    swapped = jnp.where(near, swapped3[...], swapped_facing[...])
    at0 = pl.ds(pl.multiple_of(where[3] * WIDE, WIDE), WIDE)
    at1 = pl.ds(pl.multiple_of((1 - where[3]) * WIDE, WIDE), WIDE)
    products(rows, swapped, ((b0, scale0, at0), (b1, scale1, at1)), where[2], out)


def last_call(where, rows, first, second, before):
    def place_out(step, where):
        return 0, z_of(step, where), 1 - where[1], 0, 0, 0

    vmem, anywhere = pl.BlockSpec(memory_space=pltpu.VMEM), pl.BlockSpec(memory_space=pl.ANY)
    of_three = pl.BlockSpec((SHARD, SPEC), lambda step, where: (jnp.minimum(step, 2), 0))
    of_three_swapped = pl.BlockSpec(
        (SHARD, SPEC), lambda step, where: (jnp.where(step == 1, 2, jnp.where(step == 2, 1, 2 * (step // 3))), 0)
    )
    whole = pl.BlockSpec((SHARD, SPEC), lambda step, where: (0, 0))
    return pl.pallas_call(
        last_kernel,
        grid_spec=pltpu.PrefetchScalarGridSpec(
            num_scalar_prefetch=1,
            grid=(4,),
            in_specs=[of_three, whole, of_three_swapped, whole, vmem, vmem, vmem, vmem, anywhere],
            out_specs=pl.BlockSpec((2, 1, 1, 2, SHARD, COLS), place_out),
        ),
        out_shape=jax.ShapeDtypeStruct(OUT, F32),
        input_output_aliases={9: 0},
        compiler_params=pltpu.CompilerParams(vmem_limit_bytes=16 * 2**20),
        cost_estimate=pl.CostEstimate(flops=2**32, bytes_accessed=12 * 2**20, transcendentals=2048),
        name="across_rows",
    )(where, *rows, *first, *second, before)


def in_hbm(value):
    return pltpu.with_memory_space_constraint(value, pltpu.HBM)


def stack(*values):
    return jnp.stack(values).astype(jnp.int32)


def together(*values):
    return lax.optimization_barrier(values)


def family(*shards):
    return jnp.concatenate(shards, axis=0)


def by_z(z, *placed):
    rows = jnp.zeros((4 * SHARD, SPEC), BF16)
    for shard, up in placed:
        rows = lax.dynamic_update_slice(rows, shard, ((z + up) % 4 * SHARD, 0))
    return rows


def shards(x):
    row, col = lax.axis_index("row"), lax.axis_index("col")
    low, y, z, high, core = row % 2, row // 2, col // 4, col // 2 % 2, col % 2

    def places(half, *steps):
        return stack(z, high, core, half, *[piece_spot((y + up) % 4, z, core, hx) % 4 for up, hx in steps])

    near_half = (y - z + 3) % 2
    one, two = 3 - 2 * core, 1 + 2 * core
    where = places(near_half, (one, low), (one, 1 - low), (two, low), (two, 1 - low))
    where_far = places(1 - near_half, (0, low), (0, 1 - low), (2, low), (2, 1 - low))
    a0, across, b0 = send(x, COLS_A), send(x, ACROSS_X), send(x, COLS_B)
    z_first, z_second = send(x, Z_FIRST), send(x, Z_SECOND)
    a0, b0 = together(a0, b0)
    own = family(a0, b0)
    y_first, y_second = send(own, Y_FIRST), send(own, Y_SECOND)
    facing = send(z_first, Z_FIRST)
    across_first, across_second = send(across, Z_FIRST), send(across, Z_SECOND)
    rows_across = family(across, across_first, across_second)
    y_first, y_second, facing, rows_across, across_first = together(y_first, y_second, facing, rows_across, across_first)
    far = send(y_first, Y_FIRST)
    rows = by_z(z, (x, 0), (z_first, one), (z_second, two), (facing, 2))
    swapped = send(rows, SWAP_CORE)
    facing_across = send(across_first, Z_FIRST)
    out, *first = half_call(where, rows, swapped, (y_first, y_second), None, "own_rows_near")
    out, facing_across, far = together(out, facing_across, far)
    swapped_across = send(rows_across, SWAP_CORE)
    facing_swapped = send(facing_across, SWAP_CORE)
    out, *second = half_call(where_far, rows, swapped, (own, far), out, "own_rows_far")
    out = last_call(where, (rows_across, facing_across, swapped_across, facing_swapped), first, second, out)
    return out.reshape(2, 4 * 4 * SHARD, COLS)


def solution(mesh):
    return jax.shard_map(
        shards, mesh=mesh, in_specs=(P(AXES, None),), out_specs=P(None, "row", "col"), check_vma=False
    )
```

```python
import jax
import jax.numpy as jnp
from jax import lax
from jax.experimental import pallas as pl
from jax.experimental.pallas import tpu as pltpu
from jax.sharding import PartitionSpec as P

TAPERS = 8
BINS = 64
HALF = TAPERS * BINS
SPEC = 2 * HALF
AXES = ("row", "col")
NT = (((1,), (1,)), ((), ()))
F32, BF16 = jnp.float32, jnp.bfloat16
SHARD = 128
COLS = 8 * SHARD
WIDE = COLS // 2
OUT = (2, 4, 2, 2, SHARD, COLS)
TILE = 2 * SHARD


def place(i):
    row, col = divmod(i, 16)
    return (col // 2 % 2) * 2 + row % 2, row // 2, col // 4, col % 2


def number(x, y, z, core):
    return (y * 2 + x % 2) * 16 + z * 4 + (x // 2) * 2 + core


def moves(rule):
    return [(i, number(*rule(*place(i)))) for i in range(128)]


SWAP_CORE = moves(lambda x, y, z, c: (x, y, z, 1 - c))
Y_FIRST = moves(lambda x, y, z, c: (x, (y + 1 + 2 * c) % 4, z, c))
Y_SECOND = moves(lambda x, y, z, c: (x, (y + 3 + 2 * c) % 4, z, c))
Z_FIRST = moves(lambda x, y, z, c: (x, y, (z + 1 + 2 * c) % 4, c))
Z_FIRST_CROSS = moves(lambda x, y, z, c: (x, y, (z + 1 + 2 * c) % 4, 1 - c))
Z_SECOND = moves(lambda x, y, z, c: (x, y, (z + 3 + 2 * c) % 4, c))
ACROSS_X = moves(lambda x, y, z, c: ((x + 2) % 4, y, z, c))


def to_columns(flip):
    def rule(x, y, z, c):
        return 2 * (x % 2) + (x // 2 ^ flip), (y + z + 2 * c) % 4, y, z // 2

    return moves(rule)


COLS_A, COLS_B = to_columns(0), to_columns(1)


def piece_spot(y, z, core, high):
    low_z = (y - z + 4) % 2
    from_core = ((y - z - low_z + 8) // 2 + core) % 2
    return low_z * 4 + high * 2 + from_core


def send(value, pairs):
    return lax.ppermute(value, AXES, pairs)


def column_scale(b):
    squares = jnp.zeros((WIDE, 128), F32)
    for n in range(0, SPEC, 128):
        values = b[:, n : n + 128].astype(F32)
        squares += values * values
    power = lax.dot_general(
        jnp.ones((8, 128), F32), squares, NT, precision=lax.Precision.HIGHEST, preferred_element_type=F32
    )
    return 1.0 / jnp.sqrt(power)


def products(rows, swapped, columns, core, out):
    a = jnp.concatenate([rows, swapped], axis=0)
    turned = jnp.concatenate([a[:, HALF:], -a[:, :HALF]], axis=1)
    values = a.astype(F32)
    row_inv = 1.0 / jnp.sqrt(jnp.sum(values * values, axis=1, keepdims=True))
    for b, col_inv, at in columns:
        for part, lhs in enumerate((a, turned)):
            cross = lax.dot_general(lhs, b[...], NT, preferred_element_type=F32)
            scaled = cross * row_inv * col_inv[0:1, :]
            n = rows.shape[0] // SHARD
            out[part, :, 0, core, :, at] = scaled[: n * SHARD].reshape(n, SHARD, -1)
            out[part, :, 0, 1 - core, :, at] = scaled[n * SHARD :].reshape(n, SHARD, -1)


def half_kernel(where, rows, swapped, *refs):
    out, b, col_inv, sems = refs[-4:]
    pieces = [ref.at[pl.ds(n, SHARD)] for ref in refs[:-4] if len(ref.shape) == 2 for n in range(0, ref.shape[0], SHARD)]

    @pl.when(pl.program_id(0) == 0)
    def _():
        spots = [pl.ds(pl.multiple_of(where[4 + n] * SHARD, SHARD), SHARD) for n in range(4)]
        copies = [pltpu.make_async_copy(pieces[n], b.at[spots[n], :], sems.at[n]) for n in range(4)]
        for copy in copies:
            copy.start()
        for copy in copies:
            copy.wait()
        col_inv[...] = column_scale(b)

    products(rows[...], swapped[...], ((b, col_inv, slice(None)),), where[2], out)


def z_of(step, where):
    first = 3 - 2 * where[2]
    return lax.rem(where[0] + jnp.where(step == 1, first, jnp.where(step == 2, 4 - first, 2 * (step // 3))), 4)


def half_call(where, rows, swapped, pieces, before, name):
    def place_out(step, where):
        return 0, step, where[1], 0, 0, where[3]

    pair = pl.BlockSpec((TILE, SPEC), lambda step, where: (step, 0))
    vmem, anywhere = pl.BlockSpec(memory_space=pltpu.VMEM), pl.BlockSpec(memory_space=pl.ANY)
    in_specs = [pair, pair] + [anywhere] * len(pieces)
    operands, aliases = (rows, swapped, *[in_hbm(piece) for piece in pieces]), {}
    if before is not None:
        aliases = {1 + len(operands): 0}
        operands = (*operands, before)
        in_specs.append(anywhere)
    return pl.pallas_call(
        half_kernel,
        grid_spec=pltpu.PrefetchScalarGridSpec(
            num_scalar_prefetch=1,
            grid=(2,),
            in_specs=in_specs,
            out_specs=[pl.BlockSpec((2, 2, 1, 2, SHARD, WIDE), place_out), vmem, vmem],
            scratch_shapes=[pltpu.SemaphoreType.DMA((4,))],
        ),
        out_shape=[
            jax.ShapeDtypeStruct(OUT, F32),
            (pltpu.HBM if before is None else jax.ShapeDtypeStruct)((WIDE, SPEC), BF16),
            jax.ShapeDtypeStruct((8, WIDE), F32),
        ],
        input_output_aliases=aliases,
        compiler_params=pltpu.CompilerParams(vmem_limit_bytes=16 * 2**20),
        cost_estimate=pl.CostEstimate(flops=2**31, bytes_accessed=7 * 2**20, transcendentals=2048),
        name=name,
    )(where, *operands)


def last_kernel(where, rows3, facing, swapped3, swapped_facing, b0, scale0, b1, scale1, before, out):
    near = pl.program_id(0) < 3
    rows = jnp.where(near, rows3[...], facing[...])
    swapped = jnp.where(near, swapped3[...], swapped_facing[...])
    at0 = pl.ds(pl.multiple_of(where[3] * WIDE, WIDE), WIDE)
    at1 = pl.ds(pl.multiple_of((1 - where[3]) * WIDE, WIDE), WIDE)
    products(rows, swapped, ((b0, scale0, at0), (b1, scale1, at1)), where[2], out)


def last_call(where, rows, first, second, before):
    def place_out(step, where):
        return 0, z_of(step, where), 1 - where[1], 0, 0, 0

    vmem, anywhere = pl.BlockSpec(memory_space=pltpu.VMEM), pl.BlockSpec(memory_space=pl.ANY)
    of_three = pl.BlockSpec((SHARD, SPEC), lambda step, where: (jnp.minimum(step, 2), 0))
    of_three_swapped = pl.BlockSpec(
        (SHARD, SPEC), lambda step, where: (jnp.where(step == 1, 2, jnp.where(step == 2, 1, 2 * (step // 3))), 0)
    )
    whole = pl.BlockSpec((SHARD, SPEC), lambda step, where: (0, 0))
    return pl.pallas_call(
        last_kernel,
        grid_spec=pltpu.PrefetchScalarGridSpec(
            num_scalar_prefetch=1,
            grid=(4,),
            in_specs=[of_three, whole, of_three_swapped, whole, vmem, vmem, vmem, vmem, anywhere],
            out_specs=pl.BlockSpec((2, 1, 1, 2, SHARD, COLS), place_out),
        ),
        out_shape=jax.ShapeDtypeStruct(OUT, F32),
        input_output_aliases={9: 0},
        compiler_params=pltpu.CompilerParams(vmem_limit_bytes=16 * 2**20),
        cost_estimate=pl.CostEstimate(flops=2**32, bytes_accessed=12 * 2**20, transcendentals=2048),
        name="across_rows",
    )(where, *rows, *first, *second, before)


def in_hbm(value):
    return pltpu.with_memory_space_constraint(value, pltpu.HBM)


def stack(*values):
    return jnp.stack(values).astype(jnp.int32)


def together(*values):
    return lax.optimization_barrier(values)


def family(*shards):
    return jnp.concatenate(shards, axis=0)


def by_z(z, *placed):
    rows = jnp.zeros((4 * SHARD, SPEC), BF16)
    for shard, up in placed:
        rows = lax.dynamic_update_slice(rows, shard, ((z + up) % 4 * SHARD, 0))
    return rows


def shards(x):
    row, col = lax.axis_index("row"), lax.axis_index("col")
    low, y, z, high, core = row % 2, row // 2, col // 4, col // 2 % 2, col % 2

    def places(half, *steps):
        return stack(z, high, core, half, *[piece_spot((y + up) % 4, z, core, hx) % 4 for up, hx in steps])

    near_half = (y - z + 3) % 2
    one, two = 3 - 2 * core, 1 + 2 * core
    where = places(near_half, (one, low), (one, 1 - low), (two, low), (two, 1 - low))
    where_far = places(1 - near_half, (0, low), (0, 1 - low), (2, low), (2, 1 - low))
    a0, across, b0 = send(x, COLS_A), send(x, ACROSS_X), send(x, COLS_B)
    z_first, z_second = send(x, Z_FIRST), send(x, Z_SECOND)
    a0, b0 = together(a0, b0)
    own = family(a0, b0)
    y_first, y_second = send(own, Y_FIRST), send(own, Y_SECOND)
    facing = send(z_first, Z_FIRST)
    across_first, across_second = send(across, Z_FIRST), send(across, Z_SECOND)
    rows_across = family(across, across_first, across_second)
    y_first, y_second, facing, rows_across, across_first = together(y_first, y_second, facing, rows_across, across_first)
    far = send(y_first, Y_FIRST)
    rows = by_z(z, (x, 0), (z_first, one), (z_second, two), (facing, 2))
    swapped = send(rows, SWAP_CORE)
    facing_across, facing_swapped = send(across_first, Z_FIRST), send(across_first, Z_FIRST_CROSS)
    out, *first = half_call(where, rows, swapped, (y_first, y_second), None, "own_rows_near")
    out, facing_across, facing_swapped, far = together(out, facing_across, facing_swapped, far)
    swapped_across = send(rows_across, SWAP_CORE)
    out, *second = half_call(where_far, rows, swapped, (own, far), out, "own_rows_far")
    out = last_call(where, (rows_across, facing_across, swapped_across, facing_swapped), first, second, out)
    return out.reshape(2, 4 * 4 * SHARD, COLS)


def solution(mesh):
    return jax.shard_map(
        shards, mesh=mesh, in_specs=(P(AXES, None),), out_specs=P(None, "row", "col"), check_vma=False
    )
```
